32 devices in a mesh: freq: 4 (over x, core), col: 8 (over z, y).
Axes of the slice: x: 2, y: 2, z: 4, core: 2. Of those that a mesh axis runs over, the one named last changes fastest.
Arguments:
- spectra: bfloat16 [2, 8, 4096, 4096], P(None, None, 'freq', 'col'), may hold values from -0.62890625 to 0.62890625
- wavelet: float32 [2, 8], P(None, 'freq'), may hold values from -1.5 to 1.5
Outputs:
- predicted: bfloat16 [2, 8, 384, 4096], P(None, 'freq', None, 'col')
The draws below stay inside these ranges and needn't reach their ends.
All inputs are finite; a program needn't handle non-finite values.
Results may differ from the reference program's by a relative error of at most 0.001.
Values may be sent and summed in bfloat16 or wider, within the bound.
A program may use at most 128 MiB of HBM per device.

```python
import jax
import jax.numpy as jnp
from jax import lax

NS = 4096
NOUT = 384
NF = 8


def shard_levels(rng, extent, cuts, least, high):
    level, own = 1.0, jax.random.fold_in(rng, 6)
    for dim, blocks in cuts:
        steps = jnp.exp(jax.random.uniform(jax.random.fold_in(own, dim), (blocks,), jnp.float32, least / len(cuts), high / len(cuts)))
        level = level * jnp.repeat(steps, extent[dim] // blocks).reshape([-1 if axis == dim else 1 for axis in range(len(extent))])
    return level


def scatter_about(own_key, dims, scale, limit, pieces=(), dtype=jnp.bfloat16):
    factor_of = shard_levels(own_key, dims, pieces, -0.22, 0.18) if pieces else 1.0
    values = jax.random.normal(own_key, dims, jnp.float32) * scale * factor_of
    return jnp.minimum(jnp.maximum(values, -limit), limit).astype(dtype)


def setup_inputs(seed: int = 0) -> dict:
    streams_of = jax.random.split(jax.random.key(seed), 3)
    return {
        "spectra": scatter_about(streams_of[0], (2, NF, NS, NS), 0.105, 0.62890625, ((2, 4), (3, 8))),
        "wavelet": jnp.clip(jax.random.uniform(streams_of[1], (2, NF), jnp.float32, -1.5, 1.5) * shard_levels(streams_of[1], (2, NF), ((1, 4),), -0.4, 0.0), -1.5, 1.5),
    }


def matmul_full(left, right):
    return jnp.dot(left.astype(jnp.float32), right.astype(jnp.float32), precision=lax.Precision.HIGHEST)


def single_frequency(slab):
    upper = slab[:, :NOUT, :]
    real_part = matmul_full(upper[0], slab[0]) - matmul_full(upper[1], slab[1])
    imag_part = matmul_full(upper[0], slab[1]) + matmul_full(upper[1], slab[0])
    return jnp.stack([real_part, imag_part])


def reference(spectra, wavelet):
    ordered = jnp.moveaxis(spectra, 1, 0)
    products = lax.map(single_frequency, ordered)
    products = jnp.moveaxis(products, 0, 1)
    wave_real = wavelet[0][:, None, None]
    wave_imag = wavelet[1][:, None, None]
    real_out = -(wave_real * products[0] - wave_imag * products[1])
    imag_out = -(wave_real * products[1] + wave_imag * products[0])
    return jnp.stack([real_out, imag_out]).astype(jnp.bfloat16)
```

```python
import functools

import jax
import jax.numpy as jnp
from jax import lax
from jax.experimental import pallas as pl
from jax.experimental.pallas import tpu as pltpu
from jax.sharding import PartitionSpec as P

NOUT = 384
HALVES = 2
AHEAD = 3
LAG = 6
MESH = pl.DeviceIdType.MESH


def kernel(nf, ncol, spec, wave, out, upper, data, part, pair, far, data_sem, src_send, col_recv,
           up_send, down_send, y_send, y_recv, pair_send, pair_recv, far_send, far_recv):
    own = wave.shape[1]
    freqs, shots, width = spec.shape[1], spec.shape[2], spec.shape[3]
    ny = ncol // nf
    nz, nh = nf, nf // 2
    rows = NOUT // HALVES
    chunks = freqs * HALVES
    r, c = lax.axis_index("freq"), lax.axis_index("col")
    z, y = lax.div(c, ny), lax.rem(c, ny)
    h, k = lax.div(r, 2), lax.rem(r, 2)

    def at(freq, col):
        return {"freq": freq, "col": col}

    barrier = pltpu.get_barrier_semaphore()
    for d in range(1, nf):
        pl.semaphore_signal(barrier, inc=1, device_id=at(lax.rem(r + d, nf), c), device_id_type=MESH)
    for d in range(1, ny):
        pl.semaphore_signal(
            barrier, inc=1, device_id=at(r, z * ny + lax.rem(y + d, ny)), device_id_type=MESH
        )

    @pl.when(z > 0)
    def _():
        pl.semaphore_signal(barrier, inc=1, device_id=at(r, c - ny), device_id_type=MESH)

    @pl.when(z < nz - 1)
    def _():
        pl.semaphore_signal(barrier, inc=1, device_id=at(r, c + ny), device_id_type=MESH)

    def place(t):
        group, spot = lax.div(t, nf), lax.rem(t, nf)
        hh, kk = lax.rem(spot, nh), lax.div(spot, nh)
        f = (hh * 2 + kk) * own + lax.div(group, HALVES)
        return group, lax.rem(group, HALVES), hh, kk, f

    def source(t):
        _, half, _, _, f = place(t)
        return spec.at[:, f, pl.ds(pl.multiple_of(half * rows, rows), rows), :]

    def remote(src, dst, send, recv, device):
        return pltpu.make_async_remote_copy(
            src_ref=src, dst_ref=dst, send_sem=send, recv_sem=recv, device_id=device, device_id_type=MESH
        )

    def local_copy(t):
        return pltpu.make_async_copy(source(t), upper.at[y, t], col_recv.at[t])

    def source_copy(t):
        return remote(source(t), upper.at[y, t], src_send.at[t], col_recv.at[t], at(z, c))

    def up_copy(t):
        return remote(upper.at[y, t], upper.at[y, t], up_send.at[t], col_recv.at[t], at(r, c + ny))

    def down_copy(t):
        return remote(upper.at[y, t], upper.at[y, t], down_send.at[t], col_recv.at[t], at(r, c - ny))

    def y_copy(t, d):
        to = at(r, z * ny + lax.rem(y + d, ny))
        return remote(upper.at[y, t], upper.at[y, t], y_send.at[d - 1, t], y_recv.at[d - 1, t], to)

    def y_arrival(t, d):
        origin = lax.rem(y - d + ny, ny)
        block = upper.at[origin, t]
        return remote(block, block, y_send.at[d - 1, t], y_recv.at[d - 1, t], at(r, z * ny + origin))

    def pair_copy(t):
        group, _, hh, kk, _ = place(t)
        slot = group * nh + hh
        return remote(part.at[t], pair.at[slot], pair_send.at[t], pair_recv.at[slot], at(h * 2 + kk, c))

    def pair_arrival(t):
        group, _, hh, _, _ = place(t)
        slot = group * nh + hh
        return remote(part.at[t], pair.at[slot], pair_send.at[t], pair_recv.at[slot], at(h * 2 + 1 - k, c))

    def far_copy(t):
        group, _, hh, kk, _ = place(t)
        d = lax.rem(h - hh + nh, nh) - 1
        return remote(part.at[t], far.at[d, group], far_send.at[t], far_recv.at[d, group], at(hh * 2 + kk, c))

    def far_arrival(t, d):
        group, _, hh, kk, _ = place(t)
        origin = lax.rem(h + d + 1, nh) * 2 + k
        return remote(part.at[t], far.at[d, group], far_send.at[t], far_recv.at[d, group], at(origin, c))

    local_root = (r == 0) & (z == 0)
    sends_source = (r == 0) & (z > 0)
    goes_up = (z >= r) & (z < nz - 1)
    goes_down = (z <= r) & (z > 0)

    def start_source(t):
        @pl.when(local_root)
        def _():
            local_copy(t).start()

        @pl.when(sends_source)
        def _():
            source_copy(t).start()

    count = (nf - 1) + (ny - 1) + (z > 0).astype(jnp.int32) + (z < nz - 1).astype(jnp.int32)
    pl.semaphore_wait(barrier, count)

    for t in range(AHEAD):
        start_source(t)

    def load(f):
        return pltpu.make_async_copy(spec.at[:, f], data.at[f], data_sem.at[f])

    @pl.loop(0, freqs)
    def _(i):
        load(place(lax.rem(i, nf) + lax.div(i, nf) * nf * HALVES)[4]).start()

    def arrive(t):
        @pl.when(local_root)
        def _():
            local_copy(t).wait()

        @pl.when(jnp.logical_not(local_root))
        def _():
            down_copy(t).wait_recv()

        @pl.when(goes_up)
        def _():
            up_copy(t).start()

        @pl.when(goes_down)
        def _():
            down_copy(t).start()

        for d in range(1, ny):
            y_copy(t, d).start()

    def sent(t):
        @pl.when(sends_source)
        def _():
            source_copy(t).wait_send()

        @pl.when(goes_up)
        def _():
            up_copy(t).wait_send()

        @pl.when(goes_down)
        def _():
            down_copy(t).wait_send()

        for d in range(1, ny):
            y_copy(t, d).wait_send()

    def multiply(t):
        _, half, _, kk, f = place(t)
        for d in range(1, ny):
            y_arrival(t, d).wait_recv()

        @pl.when(half == 0)
        def _():
            load(f).wait()

        def dot(a, b):
            return jnp.dot(a, b, preferred_element_type=jnp.float32)

        tile = min(256, width)

        @pl.loop(0, width // tile)
        def _(j):
            columns = pl.ds(pl.multiple_of(j * tile, tile), tile)
            real, imag = None, None
            for b in range(ny):
                depth = slice(b * width, (b + 1) * width)
                ur, ui = upper[b, t, 0], upper[b, t, 1]
                dr, di = data[f, 0, depth, columns], data[f, 1, depth, columns]
                re = dot(ur, dr) - dot(ui, di)
                im = dot(ur, di) + dot(ui, dr)
                real = re if real is None else real + re
                imag = im if imag is None else imag + im
            part[t, 0, :, columns] = real
            part[t, 1, :, columns] = imag

        @pl.when(kk != k)
        def _():
            pair_copy(t).start()

    def join(t):
        group, _, hh, kk, _ = place(t)

        @pl.when(kk == k)
        def _():
            pair_arrival(t).wait_recv()
            part[t] = part[t] + pair[group * nh + hh]

            @pl.when(hh != h)
            def _():
                far_copy(t).start()

    def finish(t):
        group, half, hh, kk, _ = place(t)

        @pl.when(kk != k)
        def _():
            pair_copy(t).wait_send()

        @pl.when((kk == k) & (hh != h))
        def _():
            far_copy(t).wait_send()

        @pl.when((kk == k) & (hh == h))
        def _():
            for d in range(nh - 1):
                far_arrival(t, d).wait_recv()
            real, imag = part[t, 0], part[t, 1]
            for d in range(nh - 1):
                real = real + far[d, group, 0]
                imag = imag + far[d, group, 1]
            j = lax.div(group, HALVES)
            wr, wi = wave[0, j], wave[1, j]
            where = pl.ds(pl.multiple_of(half * rows, rows), rows)
            out[0, j, where, :] = (-(wr * real - wi * imag)).astype(out.dtype)
            out[1, j, where, :] = (-(wr * imag + wi * real)).astype(out.dtype)

    def within(t, fn):
        @pl.when((t >= 0) & (t < chunks))
        def _():
            fn(t)

    @pl.loop(0, chunks + LAG)
    def _(t):
        within(t - AHEAD, sent)

        @pl.when((t >= 1) & (t + AHEAD - 1 < chunks))
        def _():
            start_source(t + AHEAD - 1)

        within(t, arrive)
        within(t - 1, multiply)
        within(t - 2, join)
        within(t - LAG, finish)


def local(nf, ncol, spectra, wavelet):
    _, freqs, shots, width = spectra.shape
    own = wavelet.shape[1]
    rows, chunks = NOUT // HALVES, freqs * HALVES
    ny, nh = ncol // nf, nf // 2
    block = (2, rows, width)
    dma = pltpu.SemaphoreType.DMA
    return pl.pallas_call(
        functools.partial(kernel, nf, ncol),
        out_shape=jax.ShapeDtypeStruct((2, own, NOUT, width), jnp.bfloat16),
        in_specs=[pl.BlockSpec(memory_space=pl.ANY), pl.BlockSpec(memory_space=pltpu.SMEM)],
        out_specs=pl.BlockSpec(memory_space=pltpu.VMEM),
        scratch_shapes=[
            pltpu.VMEM((ny, chunks) + block, jnp.bfloat16),
            pltpu.VMEM((freqs, 2, shots, width), jnp.bfloat16),
            pltpu.VMEM((chunks,) + block, jnp.float32),
            pltpu.VMEM((chunks // 2,) + block, jnp.float32),
            pltpu.VMEM((nh - 1, chunks // nf) + block, jnp.float32),
            dma((freqs,)),
            dma((chunks,)),
            dma((chunks,)),
            dma((chunks,)),
            dma((chunks,)),
            dma((ny - 1, chunks)),
            dma((ny - 1, chunks)),
            dma((chunks,)),
            dma((chunks // 2,)),
            dma((chunks,)),
            dma((nh - 1, chunks // nf)),
        ],
        compiler_params=pltpu.CompilerParams(
            collective_id=0, has_side_effects=True, vmem_limit_bytes=58 * 2**20
        ),
        cost_estimate=pl.CostEstimate(
            flops=16 * freqs * NOUT * shots * width // 2, bytes_accessed=4 * freqs * shots * width, transcendentals=0
        ),
    )(spectra, wavelet)


def solution(mesh):
    return jax.shard_map(
        functools.partial(local, mesh.shape["freq"], mesh.shape["col"]),
        mesh=mesh,
        in_specs=(P(None, None, "freq", "col"), P(None, "freq")),
        out_specs=P(None, "freq", None, "col"),
        check_vma=False,
    )
```

```python
import functools

import jax
import jax.numpy as jnp
from jax import lax
from jax.experimental import pallas as pl
from jax.experimental.pallas import tpu as pltpu
from jax.sharding import PartitionSpec as P

NOUT = 384
HALVES = 4
AHEAD = 6
LAG = 11
MESH = pl.DeviceIdType.MESH


def kernel(nf, ncol, spec, wave, out, upper, data, part, pair, far, data_sem, src_send, col_recv,
           up_send, down_send, y_send, y_recv, pair_send, pair_recv, far_send, far_recv):
    own = wave.shape[1]
    freqs, shots, width = spec.shape[1], spec.shape[2], spec.shape[3]
    ny = ncol // nf
    nz, nh = nf, nf // 2
    rows = NOUT // HALVES
    chunks = freqs * HALVES
    r, c = lax.axis_index("freq"), lax.axis_index("col")
    z, y = lax.div(c, ny), lax.rem(c, ny)
    h, k = lax.div(r, 2), lax.rem(r, 2)

    def at(freq, col):
        return {"freq": freq, "col": col}

    barrier = pltpu.get_barrier_semaphore()
    for d in range(1, nf):
        pl.semaphore_signal(barrier, inc=1, device_id=at(lax.rem(r + d, nf), c), device_id_type=MESH)
    for d in range(1, ny):
        pl.semaphore_signal(
            barrier, inc=1, device_id=at(r, z * ny + lax.rem(y + d, ny)), device_id_type=MESH
        )

    @pl.when(z > 0)
    def _():
        pl.semaphore_signal(barrier, inc=1, device_id=at(r, c - ny), device_id_type=MESH)

    @pl.when(z < nz - 1)
    def _():
        pl.semaphore_signal(barrier, inc=1, device_id=at(r, c + ny), device_id_type=MESH)

    def place(t):
        group, spot = lax.div(t, nf), lax.rem(t, nf)
        hh, kk = lax.rem(spot, nh), lax.div(spot, nh)
        f = (hh * 2 + kk) * own + lax.div(group, HALVES)
        return group, lax.rem(group, HALVES), hh, kk, f

    def source(t):
        _, half, _, _, f = place(t)
        return spec.at[:, f, pl.ds(pl.multiple_of(half * rows, rows), rows), :]

    def remote(src, dst, send, recv, device):
        return pltpu.make_async_remote_copy(
            src_ref=src, dst_ref=dst, send_sem=send, recv_sem=recv, device_id=device, device_id_type=MESH
        )

    def local_copy(t):
        return pltpu.make_async_copy(source(t), upper.at[y, t], col_recv.at[t])

    def source_copy(t):
        return remote(source(t), upper.at[y, t], src_send.at[t], col_recv.at[t], at(z, c))

    def up_copy(t):
        return remote(upper.at[y, t], upper.at[y, t], up_send.at[t], col_recv.at[t], at(r, c + ny))

    def down_copy(t):
        return remote(upper.at[y, t], upper.at[y, t], down_send.at[t], col_recv.at[t], at(r, c - ny))

    def y_copy(t, d):
        to = at(r, z * ny + lax.rem(y + d, ny))
        return remote(upper.at[y, t], upper.at[y, t], y_send.at[d - 1, t], y_recv.at[d - 1, t], to)

    def y_arrival(t, d):
        origin = lax.rem(y - d + ny, ny)
        block = upper.at[origin, t]
        return remote(block, block, y_send.at[d - 1, t], y_recv.at[d - 1, t], at(r, z * ny + origin))

    def pair_copy(t):
        group, _, hh, kk, _ = place(t)
        slot = group * nh + hh
        return remote(part.at[t], pair.at[slot], pair_send.at[t], pair_recv.at[slot], at(h * 2 + kk, c))

    def pair_arrival(t):
        group, _, hh, _, _ = place(t)
        slot = group * nh + hh
        return remote(part.at[t], pair.at[slot], pair_send.at[t], pair_recv.at[slot], at(h * 2 + 1 - k, c))

    def far_copy(t):
        group, _, hh, kk, _ = place(t)
        d = lax.rem(h - hh + nh, nh) - 1
        return remote(part.at[t], far.at[d, group], far_send.at[t], far_recv.at[d, group], at(hh * 2 + kk, c))

    def far_arrival(t, d):
        group, _, hh, kk, _ = place(t)
        origin = lax.rem(h + d + 1, nh) * 2 + k
        return remote(part.at[t], far.at[d, group], far_send.at[t], far_recv.at[d, group], at(origin, c))

    local_root = (r == 0) & (z == 0)
    sends_source = (r == 0) & (z > 0)
    goes_up = (z >= r) & (z < nz - 1)
    goes_down = (z <= r) & (z > 0)

    def start_source(t):
        @pl.when(local_root)
        def _():
            local_copy(t).start()

        @pl.when(sends_source)
        def _():
            source_copy(t).start()

    count = (nf - 1) + (ny - 1) + (z > 0).astype(jnp.int32) + (z < nz - 1).astype(jnp.int32)
    pl.semaphore_wait(barrier, count)

    for t in range(AHEAD):
        start_source(t)

    def load(f):
        return pltpu.make_async_copy(spec.at[:, f], data.at[f], data_sem.at[f])

    @pl.loop(0, freqs)
    def _(i):
        load(place(lax.rem(i, nf) + lax.div(i, nf) * nf * HALVES)[4]).start()

    def arrive(t):
        @pl.when(local_root)
        def _():
            local_copy(t).wait()

        @pl.when(jnp.logical_not(local_root))
        def _():
            down_copy(t).wait_recv()

        @pl.when(goes_up)
        def _():
            up_copy(t).start()

        @pl.when(goes_down)
        def _():
            down_copy(t).start()

        for d in range(1, ny):
            y_copy(t, d).start()

    def sent(t):
        @pl.when(sends_source)
        def _():
            source_copy(t).wait_send()

        @pl.when(goes_up)
        def _():
            up_copy(t).wait_send()

        @pl.when(goes_down)
        def _():
            down_copy(t).wait_send()

        for d in range(1, ny):
            y_copy(t, d).wait_send()

    def multiply(t):
        _, half, _, kk, f = place(t)
        for d in range(1, ny):
            y_arrival(t, d).wait_recv()

        @pl.when(half == 0)
        def _():
            load(f).wait()

        def dot(a, b):
            return jnp.dot(a, b, preferred_element_type=jnp.float32)

        tile = min(256, width)

        @pl.loop(0, width // tile)
        def _(j):
            columns = pl.ds(pl.multiple_of(j * tile, tile), tile)
            real, imag = None, None
            for b in range(ny):
                depth = slice(b * width, (b + 1) * width)
                ur, ui = upper[b, t, 0], upper[b, t, 1]
                dr, di = data[f, 0, depth, columns], data[f, 1, depth, columns]
                re = dot(ur, dr) - dot(ui, di)
                im = dot(ur, di) + dot(ui, dr)
                real = re if real is None else real + re
                imag = im if imag is None else imag + im
            part[t, 0, :, columns] = real
            part[t, 1, :, columns] = imag

        @pl.when(kk != k)
        def _():
            pair_copy(t).start()

    def join(t):
        group, _, hh, kk, _ = place(t)

        @pl.when(kk == k)
        def _():
            pair_arrival(t).wait_recv()
            part[t] = part[t] + pair[group * nh + hh]

            @pl.when(hh != h)
            def _():
                far_copy(t).start()

    def finish(t):
        group, half, hh, kk, _ = place(t)

        @pl.when(kk != k)
        def _():
            pair_copy(t).wait_send()

        @pl.when((kk == k) & (hh != h))
        def _():
            far_copy(t).wait_send()

        @pl.when((kk == k) & (hh == h))
        def _():
            for d in range(nh - 1):
                far_arrival(t, d).wait_recv()
            real, imag = part[t, 0], part[t, 1]
            for d in range(nh - 1):
                real = real + far[d, group, 0]
                imag = imag + far[d, group, 1]
            j = lax.div(group, HALVES)
            wr, wi = wave[0, j], wave[1, j]
            where = pl.ds(pl.multiple_of(half * rows, rows), rows)
            out[0, j, where, :] = (-(wr * real - wi * imag)).astype(out.dtype)
            out[1, j, where, :] = (-(wr * imag + wi * real)).astype(out.dtype)

    def within(t, fn):
        @pl.when((t >= 0) & (t < chunks))
        def _():
            fn(t)

    @pl.loop(0, chunks + LAG)
    def _(t):
        within(t - AHEAD, sent)

        @pl.when((t >= 1) & (t + AHEAD - 1 < chunks))
        def _():
            start_source(t + AHEAD - 1)

        within(t, arrive)
        within(t - 1, multiply)
        within(t - 2, join)
        within(t - LAG, finish)


def local(nf, ncol, spectra, wavelet):
    _, freqs, shots, width = spectra.shape
    own = wavelet.shape[1]
    rows, chunks = NOUT // HALVES, freqs * HALVES
    ny, nh = ncol // nf, nf // 2
    block = (2, rows, width)
    dma = pltpu.SemaphoreType.DMA
    return pl.pallas_call(
        functools.partial(kernel, nf, ncol),
        out_shape=jax.ShapeDtypeStruct((2, own, NOUT, width), jnp.bfloat16),
        in_specs=[pl.BlockSpec(memory_space=pl.ANY), pl.BlockSpec(memory_space=pltpu.SMEM)],
        out_specs=pl.BlockSpec(memory_space=pltpu.VMEM),
        scratch_shapes=[
            pltpu.VMEM((ny, chunks) + block, jnp.bfloat16),
            pltpu.VMEM((freqs, 2, shots, width), jnp.bfloat16),
            pltpu.VMEM((chunks,) + block, jnp.float32),
            pltpu.VMEM((chunks // 2,) + block, jnp.float32),
            pltpu.VMEM((nh - 1, chunks // nf) + block, jnp.float32),
            dma((freqs,)),
            dma((chunks,)),
            dma((chunks,)),
            dma((chunks,)),
            dma((chunks,)),
            dma((ny - 1, chunks)),
            dma((ny - 1, chunks)),
            dma((chunks,)),
            dma((chunks // 2,)),
            dma((chunks,)),
            dma((nh - 1, chunks // nf)),
        ],
        compiler_params=pltpu.CompilerParams(
            collective_id=0, has_side_effects=True, vmem_limit_bytes=58 * 2**20
        ),
        cost_estimate=pl.CostEstimate(
            flops=16 * freqs * NOUT * shots * width // 2, bytes_accessed=4 * freqs * shots * width, transcendentals=0
        ),
    )(spectra, wavelet)


def solution(mesh):
    return jax.shard_map(
        functools.partial(local, mesh.shape["freq"], mesh.shape["col"]),
        mesh=mesh,
        in_specs=(P(None, None, "freq", "col"), P(None, "freq")),
        out_specs=P(None, "freq", None, "col"),
        check_vma=False,
    )
```

```python
import functools

import jax
import jax.numpy as jnp
from jax import lax
from jax.experimental import pallas as pl
from jax.experimental.pallas import tpu as pltpu
from jax.sharding import PartitionSpec as P

NOUT = 384
HALVES = 6
AHEAD = 4
LAG = 10
MESH = pl.DeviceIdType.MESH


def kernel(nf, ncol, spec, wave, out, upper, data, part, pair, far, data_sem, src_send, col_recv,
           up_send, down_send, y_send, y_recv, pair_send, pair_recv, far_send, far_recv):
    own = wave.shape[1]
    freqs, shots, width = spec.shape[1], spec.shape[2], spec.shape[3]
    ny = ncol // nf
    nz, nh = nf, nf // 2
    rows = NOUT // HALVES
    chunks = freqs * HALVES
    r, c = lax.axis_index("freq"), lax.axis_index("col")
    z, y = lax.div(c, ny), lax.rem(c, ny)
    h, k = lax.div(r, 2), lax.rem(r, 2)

    def at(freq, col):
        return {"freq": freq, "col": col}

    barrier = pltpu.get_barrier_semaphore()
    for d in range(1, nf):
        pl.semaphore_signal(barrier, inc=1, device_id=at(lax.rem(r + d, nf), c), device_id_type=MESH)
    for d in range(1, ny):
        pl.semaphore_signal(
            barrier, inc=1, device_id=at(r, z * ny + lax.rem(y + d, ny)), device_id_type=MESH
        )

    @pl.when(z > 0)
    def _():
        pl.semaphore_signal(barrier, inc=1, device_id=at(r, c - ny), device_id_type=MESH)

    @pl.when(z < nz - 1)
    def _():
        pl.semaphore_signal(barrier, inc=1, device_id=at(r, c + ny), device_id_type=MESH)

    def place(t):
        group, spot = lax.div(t, nf), lax.rem(t, nf)
        hh, kk = lax.rem(spot, nh), lax.div(spot, nh)
        f = (hh * 2 + kk) * own + lax.div(group, HALVES)
        return group, lax.rem(group, HALVES), hh, kk, f

    def source(t):
        _, half, _, _, f = place(t)
        return spec.at[:, f, pl.ds(pl.multiple_of(half * rows, rows), rows), :]

    def remote(src, dst, send, recv, device):
        return pltpu.make_async_remote_copy(
            src_ref=src, dst_ref=dst, send_sem=send, recv_sem=recv, device_id=device, device_id_type=MESH
        )

    def local_copy(t):
        return pltpu.make_async_copy(source(t), upper.at[y, t], col_recv.at[t])

    def source_copy(t):
        return remote(source(t), upper.at[y, t], src_send.at[t], col_recv.at[t], at(z, c))

    def up_copy(t):
        return remote(upper.at[y, t], upper.at[y, t], up_send.at[t], col_recv.at[t], at(r, c + ny))

    def down_copy(t):
        return remote(upper.at[y, t], upper.at[y, t], down_send.at[t], col_recv.at[t], at(r, c - ny))

    def y_copy(t, d):
        to = at(r, z * ny + lax.rem(y + d, ny))
        return remote(upper.at[y, t], upper.at[y, t], y_send.at[d - 1, t], y_recv.at[d - 1, t], to)

    def y_arrival(t, d):
        origin = lax.rem(y - d + ny, ny)
        block = upper.at[origin, t]
        return remote(block, block, y_send.at[d - 1, t], y_recv.at[d - 1, t], at(r, z * ny + origin))

    def pair_copy(t):
        group, _, hh, kk, _ = place(t)
        slot = group * nh + hh
        return remote(part.at[t], pair.at[slot], pair_send.at[t], pair_recv.at[slot], at(h * 2 + kk, c))

    def pair_arrival(t):
        group, _, hh, _, _ = place(t)
        slot = group * nh + hh
        return remote(part.at[t], pair.at[slot], pair_send.at[t], pair_recv.at[slot], at(h * 2 + 1 - k, c))

    def far_copy(t):
        group, _, hh, kk, _ = place(t)
        d = lax.rem(h - hh + nh, nh) - 1
        return remote(part.at[t], far.at[d, group], far_send.at[t], far_recv.at[d, group], at(hh * 2 + kk, c))

    def far_arrival(t, d):
        group, _, hh, kk, _ = place(t)
        origin = lax.rem(h + d + 1, nh) * 2 + k
        return remote(part.at[t], far.at[d, group], far_send.at[t], far_recv.at[d, group], at(origin, c))

    local_root = (r == 0) & (z == 0)
    sends_source = (r == 0) & (z > 0)
    goes_up = (z >= r) & (z < nz - 1)
    goes_down = (z <= r) & (z > 0)

    def start_source(t):
        @pl.when(local_root)
        def _():
            local_copy(t).start()

        @pl.when(sends_source)
        def _():
            source_copy(t).start()

    count = (nf - 1) + (ny - 1) + (z > 0).astype(jnp.int32) + (z < nz - 1).astype(jnp.int32)
    pl.semaphore_wait(barrier, count)

    for t in range(AHEAD):
        start_source(t)

    def load(f):
        return pltpu.make_async_copy(spec.at[:, f], data.at[f], data_sem.at[f])

    @pl.loop(0, freqs)
    def _(i):
        load(place(lax.rem(i, nf) + lax.div(i, nf) * nf * HALVES)[4]).start()

    def arrive(t):
        @pl.when(local_root)
        def _():
            local_copy(t).wait()

        @pl.when(jnp.logical_not(local_root))
        def _():
            down_copy(t).wait_recv()

        @pl.when(goes_up)
        def _():
            up_copy(t).start()

        @pl.when(goes_down)
        def _():
            down_copy(t).start()

        for d in range(1, ny):
            y_copy(t, d).start()

    def sent(t):
        @pl.when(sends_source)
        def _():
            source_copy(t).wait_send()

        @pl.when(goes_up)
        def _():
            up_copy(t).wait_send()

        @pl.when(goes_down)
        def _():
            down_copy(t).wait_send()

        for d in range(1, ny):
            y_copy(t, d).wait_send()

    def multiply(t):
        _, half, _, kk, f = place(t)
        for d in range(1, ny):
            y_arrival(t, d).wait_recv()

        @pl.when(half == 0)
        def _():
            load(f).wait()

        def dot(a, b):
            return jnp.dot(a, b, preferred_element_type=jnp.float32)

        tile = min(256, width)

        @pl.loop(0, width // tile)
        def _(j):
            columns = pl.ds(pl.multiple_of(j * tile, tile), tile)
            real, imag = None, None
            for b in range(ny):
                depth = slice(b * width, (b + 1) * width)
                ur, ui = upper[b, t, 0], upper[b, t, 1]
                dr, di = data[f, 0, depth, columns], data[f, 1, depth, columns]
                re = dot(ur, dr) - dot(ui, di)
                im = dot(ur, di) + dot(ui, dr)
                real = re if real is None else real + re
                imag = im if imag is None else imag + im
            part[t, 0, :, columns] = real
            part[t, 1, :, columns] = imag

        @pl.when(kk != k)
        def _():
            pair_copy(t).start()

    def join(t):
        group, _, hh, kk, _ = place(t)

        @pl.when(kk == k)
        def _():
            pair_arrival(t).wait_recv()
            part[t] = part[t] + pair[group * nh + hh]

            @pl.when(hh != h)
            def _():
                far_copy(t).start()

    def finish(t):
        group, half, hh, kk, _ = place(t)

        @pl.when(kk != k)
        def _():
            pair_copy(t).wait_send()

        @pl.when((kk == k) & (hh != h))
        def _():
            far_copy(t).wait_send()

        @pl.when((kk == k) & (hh == h))
        def _():
            for d in range(nh - 1):
                far_arrival(t, d).wait_recv()
            real, imag = part[t, 0], part[t, 1]
            for d in range(nh - 1):
                real = real + far[d, group, 0]
                imag = imag + far[d, group, 1]
            j = lax.div(group, HALVES)
            wr, wi = wave[0, j], wave[1, j]
            where = pl.ds(pl.multiple_of(half * rows, rows), rows)
            out[0, j, where, :] = (-(wr * real - wi * imag)).astype(out.dtype)
            out[1, j, where, :] = (-(wr * imag + wi * real)).astype(out.dtype)

    def within(t, fn):
        @pl.when((t >= 0) & (t < chunks))
        def _():
            fn(t)

    @pl.loop(0, chunks + LAG)
    def _(t):
        within(t - AHEAD, sent)

        @pl.when((t >= 1) & (t + AHEAD - 1 < chunks))
        def _():
            start_source(t + AHEAD - 1)

        within(t, arrive)
        within(t - 1, multiply)
        within(t - 2, join)
        within(t - LAG, finish)


def local(nf, ncol, spectra, wavelet):
    _, freqs, shots, width = spectra.shape
    own = wavelet.shape[1]
    rows, chunks = NOUT // HALVES, freqs * HALVES
    ny, nh = ncol // nf, nf // 2
    block = (2, rows, width)
    dma = pltpu.SemaphoreType.DMA
    return pl.pallas_call(
        functools.partial(kernel, nf, ncol),
        out_shape=jax.ShapeDtypeStruct((2, own, NOUT, width), jnp.bfloat16),
        in_specs=[pl.BlockSpec(memory_space=pl.ANY), pl.BlockSpec(memory_space=pltpu.SMEM)],
        out_specs=pl.BlockSpec(memory_space=pltpu.VMEM),
        scratch_shapes=[
            pltpu.VMEM((ny, chunks) + block, jnp.bfloat16),
            pltpu.VMEM((freqs, 2, shots, width), jnp.bfloat16),
            pltpu.VMEM((chunks,) + block, jnp.float32),
            pltpu.VMEM((chunks // 2,) + block, jnp.float32),
            pltpu.VMEM((nh - 1, chunks // nf) + block, jnp.float32),
            dma((freqs,)),
            dma((chunks,)),
            dma((chunks,)),
            dma((chunks,)),
            dma((chunks,)),
            dma((ny - 1, chunks)),
            dma((ny - 1, chunks)),
            dma((chunks,)),
            dma((chunks // 2,)),
            dma((chunks,)),
            dma((nh - 1, chunks // nf)),
        ],
        compiler_params=pltpu.CompilerParams(
            collective_id=0, has_side_effects=True, vmem_limit_bytes=58 * 2**20
        ),
        cost_estimate=pl.CostEstimate(
            flops=16 * freqs * NOUT * shots * width // 2, bytes_accessed=4 * freqs * shots * width, transcendentals=0
        ),
    )(spectra, wavelet)


def solution(mesh):
    return jax.shard_map(
        functools.partial(local, mesh.shape["freq"], mesh.shape["col"]),
        mesh=mesh,
        in_specs=(P(None, None, "freq", "col"), P(None, "freq")),
        out_specs=P(None, "freq", None, "col"),
        check_vma=False,
    )
```

```python
import functools

import jax
import jax.numpy as jnp
from jax import lax
from jax.experimental import pallas as pl
from jax.experimental.pallas import tpu as pltpu
from jax.sharding import PartitionSpec as P

NOUT = 384
HALVES = 4
AHEAD = 16
LAG = 11
MESH = pl.DeviceIdType.MESH


def kernel(nf, ncol, spec, wave, out, upper, data, part, pair, far, data_sem, src_send, col_recv,
           up_send, down_send, y_send, y_recv, pair_send, pair_recv, far_send, far_recv):
    own = wave.shape[1]
    freqs, shots, width = spec.shape[1], spec.shape[2], spec.shape[3]
    ny = ncol // nf
    nz, nh = nf, nf // 2
    rows = NOUT // HALVES
    chunks = freqs * HALVES
    r, c = lax.axis_index("freq"), lax.axis_index("col")
    z, y = lax.div(c, ny), lax.rem(c, ny)
    h, k = lax.div(r, 2), lax.rem(r, 2)

    def at(freq, col):
        return {"freq": freq, "col": col}

    barrier = pltpu.get_barrier_semaphore()
    for d in range(1, nf):
        pl.semaphore_signal(barrier, inc=1, device_id=at(lax.rem(r + d, nf), c), device_id_type=MESH)
    for d in range(1, ny):
        pl.semaphore_signal(
            barrier, inc=1, device_id=at(r, z * ny + lax.rem(y + d, ny)), device_id_type=MESH
        )

    @pl.when(z > 0)
    def _():
        pl.semaphore_signal(barrier, inc=1, device_id=at(r, c - ny), device_id_type=MESH)

    @pl.when(z < nz - 1)
    def _():
        pl.semaphore_signal(barrier, inc=1, device_id=at(r, c + ny), device_id_type=MESH)

    def place(t):
        group, spot = lax.div(t, nf), lax.rem(t, nf)
        hh, kk = lax.rem(spot, nh), lax.div(spot, nh)
        f = (hh * 2 + kk) * own + lax.div(group, HALVES)
        return group, lax.rem(group, HALVES), hh, kk, f

    def source(t):
        _, half, _, _, f = place(t)
        return spec.at[:, f, pl.ds(pl.multiple_of(half * rows, rows), rows), :]

    def remote(src, dst, send, recv, device):
        return pltpu.make_async_remote_copy(
            src_ref=src, dst_ref=dst, send_sem=send, recv_sem=recv, device_id=device, device_id_type=MESH
        )

    def local_copy(t):
        return pltpu.make_async_copy(source(t), upper.at[y, t], col_recv.at[t])

    def source_copy(t):
        return remote(source(t), upper.at[y, t], src_send.at[t], col_recv.at[t], at(z, c))

    def up_copy(t):
        return remote(upper.at[y, t], upper.at[y, t], up_send.at[t], col_recv.at[t], at(r, c + ny))

    def down_copy(t):
        return remote(upper.at[y, t], upper.at[y, t], down_send.at[t], col_recv.at[t], at(r, c - ny))

    def y_copy(t, d):
        to = at(r, z * ny + lax.rem(y + d, ny))
        return remote(upper.at[y, t], upper.at[y, t], y_send.at[d - 1, t], y_recv.at[d - 1, t], to)

    def y_arrival(t, d):
        origin = lax.rem(y - d + ny, ny)
        block = upper.at[origin, t]
        return remote(block, block, y_send.at[d - 1, t], y_recv.at[d - 1, t], at(r, z * ny + origin))

    def pair_copy(t):
        group, _, hh, kk, _ = place(t)
        slot = group * nh + hh
        return remote(part.at[t], pair.at[slot], pair_send.at[t], pair_recv.at[slot], at(h * 2 + kk, c))

    def pair_arrival(t):
        group, _, hh, _, _ = place(t)
        slot = group * nh + hh
        return remote(part.at[t], pair.at[slot], pair_send.at[t], pair_recv.at[slot], at(h * 2 + 1 - k, c))

    def far_copy(t):
        group, _, hh, kk, _ = place(t)
        d = lax.rem(h - hh + nh, nh) - 1
        return remote(part.at[t], far.at[d, group], far_send.at[t], far_recv.at[d, group], at(hh * 2 + kk, c))

    def far_arrival(t, d):
        group, _, hh, kk, _ = place(t)
        origin = lax.rem(h + d + 1, nh) * 2 + k
        return remote(part.at[t], far.at[d, group], far_send.at[t], far_recv.at[d, group], at(origin, c))

    local_root = (r == 0) & (z == 0)
    sends_source = (r == 0) & (z > 0)
    goes_up = (z >= r) & (z < nz - 1)
    goes_down = (z <= r) & (z > 0)

    def start_source(t):
        @pl.when(local_root)
        def _():
            local_copy(t).start()

        @pl.when(sends_source)
        def _():
            source_copy(t).start()

    count = (nf - 1) + (ny - 1) + (z > 0).astype(jnp.int32) + (z < nz - 1).astype(jnp.int32)
    pl.semaphore_wait(barrier, count)

    for t in range(AHEAD):
        start_source(t)

    def load(f):
        return pltpu.make_async_copy(spec.at[:, f], data.at[f], data_sem.at[f])

    @pl.loop(0, freqs)
    def _(i):
        load(place(lax.rem(i, nf) + lax.div(i, nf) * nf * HALVES)[4]).start()

    def arrive(t):
        @pl.when(local_root)
        def _():
            local_copy(t).wait()

        @pl.when(jnp.logical_not(local_root))
        def _():
            down_copy(t).wait_recv()

        @pl.when(goes_up)
        def _():
            up_copy(t).start()

        @pl.when(goes_down)
        def _():
            down_copy(t).start()

        for d in range(1, ny):
            y_copy(t, d).start()

    def sent(t):
        @pl.when(sends_source)
        def _():
            source_copy(t).wait_send()

        @pl.when(goes_up)
        def _():
            up_copy(t).wait_send()

        @pl.when(goes_down)
        def _():
            down_copy(t).wait_send()

        for d in range(1, ny):
            y_copy(t, d).wait_send()

    def multiply(t):
        _, half, _, kk, f = place(t)
        for d in range(1, ny):
            y_arrival(t, d).wait_recv()

        @pl.when(half == 0)
        def _():
            load(f).wait()

        def dot(a, b):
            return jnp.dot(a, b, preferred_element_type=jnp.float32)

        tile = min(256, width)

        @pl.loop(0, width // tile)
        def _(j):
            columns = pl.ds(pl.multiple_of(j * tile, tile), tile)
            real, imag = None, None
            for b in range(ny):
                depth = slice(b * width, (b + 1) * width)
                ur, ui = upper[b, t, 0], upper[b, t, 1]
                dr, di = data[f, 0, depth, columns], data[f, 1, depth, columns]
                re = dot(ur, dr) - dot(ui, di)
                im = dot(ur, di) + dot(ui, dr)
                real = re if real is None else real + re
                imag = im if imag is None else imag + im
            part[t, 0, :, columns] = real
            part[t, 1, :, columns] = imag

        @pl.when(kk != k)
        def _():
            pair_copy(t).start()

    def join(t):
        group, _, hh, kk, _ = place(t)

        @pl.when(kk == k)
        def _():
            pair_arrival(t).wait_recv()
            part[t] = part[t] + pair[group * nh + hh]

            @pl.when(hh != h)
            def _():
                far_copy(t).start()

    def finish(t):
        group, half, hh, kk, _ = place(t)

        @pl.when(kk != k)
        def _():
            pair_copy(t).wait_send()

        @pl.when((kk == k) & (hh != h))
        def _():
            far_copy(t).wait_send()

        @pl.when((kk == k) & (hh == h))
        def _():
            for d in range(nh - 1):
                far_arrival(t, d).wait_recv()
            real, imag = part[t, 0], part[t, 1]
            for d in range(nh - 1):
                real = real + far[d, group, 0]
                imag = imag + far[d, group, 1]
            j = lax.div(group, HALVES)
            wr, wi = wave[0, j], wave[1, j]
            where = pl.ds(pl.multiple_of(half * rows, rows), rows)
            out[0, j, where, :] = (-(wr * real - wi * imag)).astype(out.dtype)
            out[1, j, where, :] = (-(wr * imag + wi * real)).astype(out.dtype)

    def within(t, fn):
        @pl.when((t >= 0) & (t < chunks))
        def _():
            fn(t)

    @pl.loop(0, chunks + max(LAG, AHEAD))
    def _(t):
        within(t - AHEAD, sent)

        @pl.when((t >= 1) & (t + AHEAD - 1 < chunks))
        def _():
            start_source(t + AHEAD - 1)

        within(t, arrive)
        within(t - 1, multiply)
        within(t - 2, join)
        within(t - LAG, finish)


def local(nf, ncol, spectra, wavelet):
    _, freqs, shots, width = spectra.shape
    own = wavelet.shape[1]
    rows, chunks = NOUT // HALVES, freqs * HALVES
    ny, nh = ncol // nf, nf // 2
    block = (2, rows, width)
    dma = pltpu.SemaphoreType.DMA
    return pl.pallas_call(
        functools.partial(kernel, nf, ncol),
        out_shape=jax.ShapeDtypeStruct((2, own, NOUT, width), jnp.bfloat16),
        in_specs=[pl.BlockSpec(memory_space=pl.ANY), pl.BlockSpec(memory_space=pltpu.SMEM)],
        out_specs=pl.BlockSpec(memory_space=pltpu.VMEM),
        scratch_shapes=[
            pltpu.VMEM((ny, chunks) + block, jnp.bfloat16),
            pltpu.VMEM((freqs, 2, shots, width), jnp.bfloat16),
            pltpu.VMEM((chunks,) + block, jnp.float32),
            pltpu.VMEM((chunks // 2,) + block, jnp.float32),
            pltpu.VMEM((nh - 1, chunks // nf) + block, jnp.float32),
            dma((freqs,)),
            dma((chunks,)),
            dma((chunks,)),
            dma((chunks,)),
            dma((chunks,)),
            dma((ny - 1, chunks)),
            dma((ny - 1, chunks)),
            dma((chunks,)),
            dma((chunks // 2,)),
            dma((chunks,)),
            dma((nh - 1, chunks // nf)),
        ],
        compiler_params=pltpu.CompilerParams(
            collective_id=0, has_side_effects=True, vmem_limit_bytes=58 * 2**20
        ),
        cost_estimate=pl.CostEstimate(
            flops=16 * freqs * NOUT * shots * width // 2, bytes_accessed=4 * freqs * shots * width, transcendentals=0
        ),
    )(spectra, wavelet)


def solution(mesh):
    return jax.shard_map(
        functools.partial(local, mesh.shape["freq"], mesh.shape["col"]),
        mesh=mesh,
        in_specs=(P(None, None, "freq", "col"), P(None, "freq")),
        out_specs=P(None, "freq", None, "col"),
        check_vma=False,
    )
```

```python
import functools

import jax
import jax.numpy as jnp
from jax import lax
from jax.experimental import pallas as pl
from jax.experimental.pallas import tpu as pltpu
from jax.sharding import PartitionSpec as P

NOUT = 384
HALVES = 4
PIECES = 2
AHEAD = 16
LAG = 11
MESH = pl.DeviceIdType.MESH


def kernel(nf, ncol, spec, wave, out, upper, data, part, pair, far, data_sem, src_send, col_recv,
           up_send, down_send, y_send, y_recv, pair_send, pair_recv, far_send, far_recv):
    own = wave.shape[1]
    freqs, shots, width = spec.shape[1], spec.shape[2], spec.shape[3]
    ny = ncol // nf
    nz, nh = nf, nf // 2
    rows = NOUT // HALVES
    chunks = freqs * HALVES
    small, pieces = rows // PIECES, chunks * PIECES
    r, c = lax.axis_index("freq"), lax.axis_index("col")
    z, y = lax.div(c, ny), lax.rem(c, ny)
    h, k = lax.div(r, 2), lax.rem(r, 2)

    def at(freq, col):
        return {"freq": freq, "col": col}

    barrier = pltpu.get_barrier_semaphore()
    for d in range(1, nf):
        pl.semaphore_signal(barrier, inc=1, device_id=at(lax.rem(r + d, nf), c), device_id_type=MESH)
    for d in range(1, ny):
        pl.semaphore_signal(
            barrier, inc=1, device_id=at(r, z * ny + lax.rem(y + d, ny)), device_id_type=MESH
        )

    @pl.when(z > 0)
    def _():
        pl.semaphore_signal(barrier, inc=1, device_id=at(r, c - ny), device_id_type=MESH)

    @pl.when(z < nz - 1)
    def _():
        pl.semaphore_signal(barrier, inc=1, device_id=at(r, c + ny), device_id_type=MESH)

    def place(t):
        group, spot = lax.div(t, nf), lax.rem(t, nf)
        hh, kk = lax.rem(spot, nh), lax.div(spot, nh)
        f = (hh * 2 + kk) * own + lax.div(group, HALVES)
        return group, lax.rem(group, HALVES), hh, kk, f

    def source(s):
        _, half, _, _, f = place(lax.div(s, PIECES))
        first = pl.multiple_of(half * rows + lax.rem(s, PIECES) * small, small)
        return spec.at[:, f, pl.ds(first, small), :]

    def piece(b, s):
        first = pl.multiple_of(lax.rem(s, PIECES) * small, small)
        return upper.at[b, lax.div(s, PIECES), :, pl.ds(first, small), :]

    def remote(src, dst, send, recv, device):
        return pltpu.make_async_remote_copy(
            src_ref=src, dst_ref=dst, send_sem=send, recv_sem=recv, device_id=device, device_id_type=MESH
        )

    def local_copy(t):
        return pltpu.make_async_copy(source(t), piece(y, t), col_recv.at[t])

    def source_copy(t):
        return remote(source(t), piece(y, t), src_send.at[t], col_recv.at[t], at(z, c))

    def up_copy(t):
        return remote(piece(y, t), piece(y, t), up_send.at[t], col_recv.at[t], at(r, c + ny))

    def down_copy(t):
        return remote(piece(y, t), piece(y, t), down_send.at[t], col_recv.at[t], at(r, c - ny))

    def y_copy(t, d):
        to = at(r, z * ny + lax.rem(y + d, ny))
        return remote(piece(y, t), piece(y, t), y_send.at[d - 1, t], y_recv.at[d - 1, t], to)

    def y_arrival(t, d):
        origin = lax.rem(y - d + ny, ny)
        block = piece(origin, t)
        return remote(block, block, y_send.at[d - 1, t], y_recv.at[d - 1, t], at(r, z * ny + origin))

    def pair_copy(t):
        group, _, hh, kk, _ = place(t)
        slot = group * nh + hh
        return remote(part.at[t], pair.at[slot], pair_send.at[t], pair_recv.at[slot], at(h * 2 + kk, c))

    def pair_arrival(t):
        group, _, hh, _, _ = place(t)
        slot = group * nh + hh
        return remote(part.at[t], pair.at[slot], pair_send.at[t], pair_recv.at[slot], at(h * 2 + 1 - k, c))

    def far_copy(t):
        group, _, hh, kk, _ = place(t)
        d = lax.rem(h - hh + nh, nh) - 1
        return remote(part.at[t], far.at[d, group], far_send.at[t], far_recv.at[d, group], at(hh * 2 + kk, c))

    def far_arrival(t, d):
        group, _, hh, kk, _ = place(t)
        origin = lax.rem(h + d + 1, nh) * 2 + k
        return remote(part.at[t], far.at[d, group], far_send.at[t], far_recv.at[d, group], at(origin, c))

    local_root = (r == 0) & (z == 0)
    sends_source = (r == 0) & (z > 0)
    goes_up = (z >= r) & (z < nz - 1)
    goes_down = (z <= r) & (z > 0)

    def start_source(t):
        @pl.when(local_root)
        def _():
            local_copy(t).start()

        @pl.when(sends_source)
        def _():
            source_copy(t).start()

    count = (nf - 1) + (ny - 1) + (z > 0).astype(jnp.int32) + (z < nz - 1).astype(jnp.int32)
    pl.semaphore_wait(barrier, count)

    for t in range(AHEAD):
        start_source(t)

    def load(f):
        return pltpu.make_async_copy(spec.at[:, f], data.at[f], data_sem.at[f])

    @pl.loop(0, freqs)
    def _(i):
        load(place(lax.rem(i, nf) + lax.div(i, nf) * nf * HALVES)[4]).start()

    def arrive(t):
        @pl.when(local_root)
        def _():
            local_copy(t).wait()

        @pl.when(jnp.logical_not(local_root))
        def _():
            down_copy(t).wait_recv()

        @pl.when(goes_up)
        def _():
            up_copy(t).start()

        @pl.when(goes_down)
        def _():
            down_copy(t).start()

        for d in range(1, ny):
            y_copy(t, d).start()

    def sent(t):
        @pl.when(sends_source)
        def _():
            source_copy(t).wait_send()

        @pl.when(goes_up)
        def _():
            up_copy(t).wait_send()

        @pl.when(goes_down)
        def _():
            down_copy(t).wait_send()

        for d in range(1, ny):
            y_copy(t, d).wait_send()

    def multiply(t):
        _, half, _, kk, f = place(t)
        for d in range(1, ny):
            for i in range(PIECES):
                y_arrival(t * PIECES + i, d).wait_recv()

        @pl.when(half == 0)
        def _():
            load(f).wait()

        def dot(a, b):
            return jnp.dot(a, b, preferred_element_type=jnp.float32)

        tile = min(256, width)

        @pl.loop(0, width // tile)
        def _(j):
            columns = pl.ds(pl.multiple_of(j * tile, tile), tile)
            real, imag = None, None
            for b in range(ny):
                depth = slice(b * width, (b + 1) * width)
                ur, ui = upper[b, t, 0], upper[b, t, 1]
                dr, di = data[f, 0, depth, columns], data[f, 1, depth, columns]
                re = dot(ur, dr) - dot(ui, di)
                im = dot(ur, di) + dot(ui, dr)
                real = re if real is None else real + re
                imag = im if imag is None else imag + im
            part[t, 0, :, columns] = real
            part[t, 1, :, columns] = imag

        @pl.when(kk != k)
        def _():
            pair_copy(t).start()

    def join(t):
        group, _, hh, kk, _ = place(t)

        @pl.when(kk == k)
        def _():
            pair_arrival(t).wait_recv()
            part[t] = part[t] + pair[group * nh + hh]

            @pl.when(hh != h)
            def _():
                far_copy(t).start()

    def finish(t):
        group, half, hh, kk, _ = place(t)

        @pl.when(kk != k)
        def _():
            pair_copy(t).wait_send()

        @pl.when((kk == k) & (hh != h))
        def _():
            far_copy(t).wait_send()

        @pl.when((kk == k) & (hh == h))
        def _():
            for d in range(nh - 1):
                far_arrival(t, d).wait_recv()
            real, imag = part[t, 0], part[t, 1]
            for d in range(nh - 1):
                real = real + far[d, group, 0]
                imag = imag + far[d, group, 1]
            j = lax.div(group, HALVES)
            wr, wi = wave[0, j], wave[1, j]
            where = pl.ds(pl.multiple_of(half * rows, rows), rows)
            out[0, j, where, :] = (-(wr * real - wi * imag)).astype(out.dtype)
            out[1, j, where, :] = (-(wr * imag + wi * real)).astype(out.dtype)

    def within(t, fn, end):
        @pl.when((t >= 0) & (t < end))
        def _():
            fn(t)

    def move(s):
        within(s - AHEAD, sent, pieces)

        @pl.when((s >= 1) & (s + AHEAD - 1 < pieces))
        def _():
            start_source(s + AHEAD - 1)

        within(s, arrive, pieces)

    @pl.loop(0, chunks + max(LAG, AHEAD // PIECES))
    def _(t):
        for i in range(PIECES - 1):
            move(t * PIECES + i)
        within(t - 1, multiply, chunks)
        move(t * PIECES + PIECES - 1)
        within(t - 2, join, chunks)
        within(t - LAG, finish, chunks)


def local(nf, ncol, spectra, wavelet):
    _, freqs, shots, width = spectra.shape
    own = wavelet.shape[1]
    rows, chunks = NOUT // HALVES, freqs * HALVES
    pieces, ny, nh = chunks * PIECES, ncol // nf, nf // 2
    block = (2, rows, width)
    dma = pltpu.SemaphoreType.DMA
    return pl.pallas_call(
        functools.partial(kernel, nf, ncol),
        out_shape=jax.ShapeDtypeStruct((2, own, NOUT, width), jnp.bfloat16),
        in_specs=[pl.BlockSpec(memory_space=pl.ANY), pl.BlockSpec(memory_space=pltpu.SMEM)],
        out_specs=pl.BlockSpec(memory_space=pltpu.VMEM),
        scratch_shapes=[
            pltpu.VMEM((ny, chunks) + block, jnp.bfloat16),
            pltpu.VMEM((freqs, 2, shots, width), jnp.bfloat16),
            pltpu.VMEM((chunks,) + block, jnp.float32),
            pltpu.VMEM((chunks // 2,) + block, jnp.float32),
            pltpu.VMEM((nh - 1, chunks // nf) + block, jnp.float32),
            dma((freqs,)),
            dma((pieces,)),
            dma((pieces,)),
            dma((pieces,)),
            dma((pieces,)),
            dma((ny - 1, pieces)),
            dma((ny - 1, pieces)),
            dma((chunks,)),
            dma((chunks // 2,)),
            dma((chunks,)),
            dma((nh - 1, chunks // nf)),
        ],
        compiler_params=pltpu.CompilerParams(
            collective_id=0, has_side_effects=True, vmem_limit_bytes=58 * 2**20
        ),
        cost_estimate=pl.CostEstimate(
            flops=16 * freqs * NOUT * shots * width // 2, bytes_accessed=4 * freqs * shots * width, transcendentals=0
        ),
    )(spectra, wavelet)


def solution(mesh):
    return jax.shard_map(
        functools.partial(local, mesh.shape["freq"], mesh.shape["col"]),
        mesh=mesh,
        in_specs=(P(None, None, "freq", "col"), P(None, "freq")),
        out_specs=P(None, "freq", None, "col"),
        check_vma=False,
    )
```

```python
import functools

import jax
import jax.numpy as jnp
from jax import lax
from jax.experimental import pallas as pl
from jax.experimental.pallas import tpu as pltpu
from jax.sharding import PartitionSpec as P

NOUT = 384
HALVES = 4
AHEAD = 16
LAG = 16
MESH = pl.DeviceIdType.MESH


def kernel(nf, ncol, spec, wave, out, upper, data, part, pair, far, data_sem, src_send, col_recv,
           up_send, down_send, y_send, y_recv, pair_send, pair_recv, far_send, far_recv):
    own = wave.shape[1]
    freqs, shots, width = spec.shape[1], spec.shape[2], spec.shape[3]
    ny = ncol // nf
    nz, nh = nf, nf // 2
    rows = NOUT // HALVES
    chunks = freqs * HALVES
    r, c = lax.axis_index("freq"), lax.axis_index("col")
    z, y = lax.div(c, ny), lax.rem(c, ny)
    h, k = lax.div(r, 2), lax.rem(r, 2)

    def at(freq, col):
        return {"freq": freq, "col": col}

    barrier = pltpu.get_barrier_semaphore()
    for d in range(1, nf):
        pl.semaphore_signal(barrier, inc=1, device_id=at(lax.rem(r + d, nf), c), device_id_type=MESH)
    for d in range(1, ny):
        pl.semaphore_signal(
            barrier, inc=1, device_id=at(r, z * ny + lax.rem(y + d, ny)), device_id_type=MESH
        )

    @pl.when(z > 0)
    def _():
        pl.semaphore_signal(barrier, inc=1, device_id=at(r, c - ny), device_id_type=MESH)

    @pl.when(z < nz - 1)
    def _():
        pl.semaphore_signal(barrier, inc=1, device_id=at(r, c + ny), device_id_type=MESH)

    def place(t):
        group, spot = lax.div(t, nf), lax.rem(t, nf)
        hh, kk = lax.rem(spot, nh), lax.div(spot, nh)
        f = (hh * 2 + kk) * own + lax.div(group, HALVES)
        return group, lax.rem(group, HALVES), hh, kk, f

    def source(t):
        _, half, _, _, f = place(t)
        return spec.at[:, f, pl.ds(pl.multiple_of(half * rows, rows), rows), :]

    def remote(src, dst, send, recv, device):
        return pltpu.make_async_remote_copy(
            src_ref=src, dst_ref=dst, send_sem=send, recv_sem=recv, device_id=device, device_id_type=MESH
        )

    def local_copy(t):
        return pltpu.make_async_copy(source(t), upper.at[y, t], col_recv.at[t])

    def source_copy(t):
        return remote(source(t), upper.at[y, t], src_send.at[t], col_recv.at[t], at(z, c))

    def up_copy(t):
        return remote(upper.at[y, t], upper.at[y, t], up_send.at[t], col_recv.at[t], at(r, c + ny))

    def down_copy(t):
        return remote(upper.at[y, t], upper.at[y, t], down_send.at[t], col_recv.at[t], at(r, c - ny))

    def y_copy(t, d):
        to = at(r, z * ny + lax.rem(y + d, ny))
        return remote(upper.at[y, t], upper.at[y, t], y_send.at[d - 1, t], y_recv.at[d - 1, t], to)

    def y_arrival(t, d):
        origin = lax.rem(y - d + ny, ny)
        block = upper.at[origin, t]
        return remote(block, block, y_send.at[d - 1, t], y_recv.at[d - 1, t], at(r, z * ny + origin))

    def pair_copy(t):
        group, _, hh, kk, _ = place(t)
        slot = group * nh + hh
        return remote(part.at[t], pair.at[slot], pair_send.at[t], pair_recv.at[slot], at(h * 2 + kk, c))

    def pair_arrival(t):
        group, _, hh, _, _ = place(t)
        slot = group * nh + hh
        return remote(part.at[t], pair.at[slot], pair_send.at[t], pair_recv.at[slot], at(h * 2 + 1 - k, c))

    def far_copy(t):
        group, _, hh, kk, _ = place(t)
        d = lax.rem(h - hh + nh, nh) - 1
        return remote(part.at[t], far.at[d, group], far_send.at[t], far_recv.at[d, group], at(hh * 2 + kk, c))

    def far_arrival(t, d):
        group, _, hh, kk, _ = place(t)
        origin = lax.rem(h + d + 1, nh) * 2 + k
        return remote(part.at[t], far.at[d, group], far_send.at[t], far_recv.at[d, group], at(origin, c))

    local_root = (r == 0) & (z == 0)
    sends_source = (r == 0) & (z > 0)
    goes_up = (z >= r) & (z < nz - 1)
    goes_down = (z <= r) & (z > 0)

    def start_source(t):
        @pl.when(local_root)
        def _():
            local_copy(t).start()

        @pl.when(sends_source)
        def _():
            source_copy(t).start()

    count = (nf - 1) + (ny - 1) + (z > 0).astype(jnp.int32) + (z < nz - 1).astype(jnp.int32)
    pl.semaphore_wait(barrier, count)

    for t in range(AHEAD):
        start_source(t)

    def load(f):
        return pltpu.make_async_copy(spec.at[:, f], data.at[f], data_sem.at[f])

    @pl.loop(0, freqs)
    def _(i):
        load(place(lax.rem(i, nf) + lax.div(i, nf) * nf * HALVES)[4]).start()

    def arrive(t):
        @pl.when(local_root)
        def _():
            local_copy(t).wait()

        @pl.when(jnp.logical_not(local_root))
        def _():
            down_copy(t).wait_recv()

        @pl.when(goes_up)
        def _():
            up_copy(t).start()

        @pl.when(goes_down)
        def _():
            down_copy(t).start()

        for d in range(1, ny):
            y_copy(t, d).start()

    def sent(t):
        @pl.when(sends_source)
        def _():
            source_copy(t).wait_send()

        @pl.when(goes_up)
        def _():
            up_copy(t).wait_send()

        @pl.when(goes_down)
        def _():
            down_copy(t).wait_send()

        for d in range(1, ny):
            y_copy(t, d).wait_send()

    def multiply(t):
        _, half, _, kk, f = place(t)
        for d in range(1, ny):
            y_arrival(t, d).wait_recv()

        @pl.when(half == 0)
        def _():
            load(f).wait()

        def dot(a, b):
            return jnp.dot(a, b, preferred_element_type=jnp.float32)

        tile = min(256, width)

        @pl.loop(0, width // tile)
        def _(j):
            columns = pl.ds(pl.multiple_of(j * tile, tile), tile)
            real, imag = None, None
            for b in range(ny):
                depth = slice(b * width, (b + 1) * width)
                ur, ui = upper[b, t, 0], upper[b, t, 1]
                dr, di = data[f, 0, depth, columns], data[f, 1, depth, columns]
                re = dot(ur, dr) - dot(ui, di)
                im = dot(ur, di) + dot(ui, dr)
                real = re if real is None else real + re
                imag = im if imag is None else imag + im
            part[t, 0, :, columns] = real
            part[t, 1, :, columns] = imag

        @pl.when(kk != k)
        def _():
            pair_copy(t).start()

    def join(t):
        group, _, hh, kk, _ = place(t)

        @pl.when(kk == k)
        def _():
            pair_arrival(t).wait_recv()
            part[t] = part[t] + pair[group * nh + hh]

            @pl.when(hh != h)
            def _():
                far_copy(t).start()

    def finish(t):
        group, half, hh, kk, _ = place(t)

        @pl.when(kk != k)
        def _():
            pair_copy(t).wait_send()

        @pl.when((kk == k) & (hh != h))
        def _():
            far_copy(t).wait_send()

        @pl.when((kk == k) & (hh == h))
        def _():
            for d in range(nh - 1):
                far_arrival(t, d).wait_recv()
            real, imag = part[t, 0], part[t, 1]
            for d in range(nh - 1):
                real = real + far[d, group, 0]
                imag = imag + far[d, group, 1]
            j = lax.div(group, HALVES)
            wr, wi = wave[0, j], wave[1, j]
            where = pl.ds(pl.multiple_of(half * rows, rows), rows)
            out[0, j, where, :] = (-(wr * real - wi * imag)).astype(out.dtype)
            out[1, j, where, :] = (-(wr * imag + wi * real)).astype(out.dtype)

    def within(t, fn):
        @pl.when((t >= 0) & (t < chunks))
        def _():
            fn(t)

    late = chunks - 4

    @pl.loop(0, chunks + max(LAG, AHEAD))
    def _(t):
        within(t - AHEAD, sent)

        @pl.when((t >= 1) & (t + AHEAD - 1 < chunks))
        def _():
            start_source(t + AHEAD - 1)

        within(t, arrive)
        within(t - 1, multiply)

        @pl.when(t < late)
        def _():
            within(t - 5, join)

        @pl.when((t >= late) & (t < late + 3))
        def _():
            for i in range(2):
                join(2 * (t - late) + late - 5 + i)

        @pl.when(t >= late + 3)
        def _():
            within(t - 2, join)

        within(t - LAG, finish)


def local(nf, ncol, spectra, wavelet):
    _, freqs, shots, width = spectra.shape
    own = wavelet.shape[1]
    rows, chunks = NOUT // HALVES, freqs * HALVES
    ny, nh = ncol // nf, nf // 2
    block = (2, rows, width)
    dma = pltpu.SemaphoreType.DMA
    return pl.pallas_call(
        functools.partial(kernel, nf, ncol),
        out_shape=jax.ShapeDtypeStruct((2, own, NOUT, width), jnp.bfloat16),
        in_specs=[pl.BlockSpec(memory_space=pl.ANY), pl.BlockSpec(memory_space=pltpu.SMEM)],
        out_specs=pl.BlockSpec(memory_space=pltpu.VMEM),
        scratch_shapes=[
            pltpu.VMEM((ny, chunks) + block, jnp.bfloat16),
            pltpu.VMEM((freqs, 2, shots, width), jnp.bfloat16),
            pltpu.VMEM((chunks,) + block, jnp.float32),
            pltpu.VMEM((chunks // 2,) + block, jnp.float32),
            pltpu.VMEM((nh - 1, chunks // nf) + block, jnp.float32),
            dma((freqs,)),
            dma((chunks,)),
            dma((chunks,)),
            dma((chunks,)),
            dma((chunks,)),
            dma((ny - 1, chunks)),
            dma((ny - 1, chunks)),
            dma((chunks,)),
            dma((chunks // 2,)),
            dma((chunks,)),
            dma((nh - 1, chunks // nf)),
        ],
        compiler_params=pltpu.CompilerParams(
            collective_id=0, has_side_effects=True, vmem_limit_bytes=58 * 2**20
        ),
        cost_estimate=pl.CostEstimate(
            flops=16 * freqs * NOUT * shots * width // 2, bytes_accessed=4 * freqs * shots * width, transcendentals=0
        ),
    )(spectra, wavelet)


def solution(mesh):
    return jax.shard_map(
        functools.partial(local, mesh.shape["freq"], mesh.shape["col"]),
        mesh=mesh,
        in_specs=(P(None, None, "freq", "col"), P(None, "freq")),
        out_specs=P(None, "freq", None, "col"),
        check_vma=False,
    )
```

```python
import functools

import jax
import jax.numpy as jnp
from jax import lax
from jax.experimental import pallas as pl
from jax.experimental.pallas import tpu as pltpu
from jax.sharding import PartitionSpec as P

NOUT = 384
HALVES = 6
AHEAD = 24
LAG = 24
MESH = pl.DeviceIdType.MESH


def kernel(nf, ncol, spec, wave, out, upper, data, part, pair, far, data_sem, src_send, col_recv,
           up_send, down_send, y_send, y_recv, pair_send, pair_recv, far_send, far_recv):
    own = wave.shape[1]
    freqs, shots, width = spec.shape[1], spec.shape[2], spec.shape[3]
    ny = ncol // nf
    nz, nh = nf, nf // 2
    rows = NOUT // HALVES
    chunks = freqs * HALVES
    r, c = lax.axis_index("freq"), lax.axis_index("col")
    z, y = lax.div(c, ny), lax.rem(c, ny)
    h, k = lax.div(r, 2), lax.rem(r, 2)

    def at(freq, col):
        return {"freq": freq, "col": col}

    barrier = pltpu.get_barrier_semaphore()
    for d in range(1, nf):
        pl.semaphore_signal(barrier, inc=1, device_id=at(lax.rem(r + d, nf), c), device_id_type=MESH)
    for d in range(1, ny):
        pl.semaphore_signal(
            barrier, inc=1, device_id=at(r, z * ny + lax.rem(y + d, ny)), device_id_type=MESH
        )

    @pl.when(z > 0)
    def _():
        pl.semaphore_signal(barrier, inc=1, device_id=at(r, c - ny), device_id_type=MESH)

    @pl.when(z < nz - 1)
    def _():
        pl.semaphore_signal(barrier, inc=1, device_id=at(r, c + ny), device_id_type=MESH)

    def place(t):
        group, spot = lax.div(t, nf), lax.rem(t, nf)
        hh, kk = lax.rem(spot, nh), lax.div(spot, nh)
        f = (hh * 2 + kk) * own + lax.div(group, HALVES)
        return group, lax.rem(group, HALVES), hh, kk, f

    def source(t):
        _, half, _, _, f = place(t)
        return spec.at[:, f, pl.ds(pl.multiple_of(half * rows, rows), rows), :]

    def remote(src, dst, send, recv, device):
        return pltpu.make_async_remote_copy(
            src_ref=src, dst_ref=dst, send_sem=send, recv_sem=recv, device_id=device, device_id_type=MESH
        )

    def local_copy(t):
        return pltpu.make_async_copy(source(t), upper.at[y, t], col_recv.at[t])

    def source_copy(t):
        return remote(source(t), upper.at[y, t], src_send.at[t], col_recv.at[t], at(z, c))

    def up_copy(t):
        return remote(upper.at[y, t], upper.at[y, t], up_send.at[t], col_recv.at[t], at(r, c + ny))

    def down_copy(t):
        return remote(upper.at[y, t], upper.at[y, t], down_send.at[t], col_recv.at[t], at(r, c - ny))

    def y_copy(t, d):
        to = at(r, z * ny + lax.rem(y + d, ny))
        return remote(upper.at[y, t], upper.at[y, t], y_send.at[d - 1, t], y_recv.at[d - 1, t], to)

    def y_arrival(t, d):
        origin = lax.rem(y - d + ny, ny)
        block = upper.at[origin, t]
        return remote(block, block, y_send.at[d - 1, t], y_recv.at[d - 1, t], at(r, z * ny + origin))

    def pair_copy(t):
        group, _, hh, kk, _ = place(t)
        slot = group * nh + hh
        return remote(part.at[t], pair.at[slot], pair_send.at[t], pair_recv.at[slot], at(h * 2 + kk, c))

    def pair_arrival(t):
        group, _, hh, _, _ = place(t)
        slot = group * nh + hh
        return remote(part.at[t], pair.at[slot], pair_send.at[t], pair_recv.at[slot], at(h * 2 + 1 - k, c))

    def far_copy(t):
        group, _, hh, kk, _ = place(t)
        d = lax.rem(h - hh + nh, nh) - 1
        return remote(part.at[t], far.at[d, group], far_send.at[t], far_recv.at[d, group], at(hh * 2 + kk, c))

    def far_arrival(t, d):
        group, _, hh, kk, _ = place(t)
        origin = lax.rem(h + d + 1, nh) * 2 + k
        return remote(part.at[t], far.at[d, group], far_send.at[t], far_recv.at[d, group], at(origin, c))

    local_root = (r == 0) & (z == 0)
    sends_source = (r == 0) & (z > 0)
    goes_up = (z >= r) & (z < nz - 1)
    goes_down = (z <= r) & (z > 0)

    def start_source(t):
        @pl.when(local_root)
        def _():
            local_copy(t).start()

        @pl.when(sends_source)
        def _():
            source_copy(t).start()

    count = (nf - 1) + (ny - 1) + (z > 0).astype(jnp.int32) + (z < nz - 1).astype(jnp.int32)
    pl.semaphore_wait(barrier, count)

    for t in range(AHEAD):
        start_source(t)

    def load(f):
        return pltpu.make_async_copy(spec.at[:, f], data.at[f], data_sem.at[f])

    @pl.loop(0, freqs)
    def _(i):
        load(place(lax.rem(i, nf) + lax.div(i, nf) * nf * HALVES)[4]).start()

    def arrive(t):
        @pl.when(local_root)
        def _():
            local_copy(t).wait()

        @pl.when(jnp.logical_not(local_root))
        def _():
            down_copy(t).wait_recv()

        @pl.when(goes_up)
        def _():
            up_copy(t).start()

        @pl.when(goes_down)
        def _():
            down_copy(t).start()

        for d in range(1, ny):
            y_copy(t, d).start()

    def sent(t):
        @pl.when(sends_source)
        def _():
            source_copy(t).wait_send()

        @pl.when(goes_up)
        def _():
            up_copy(t).wait_send()

        @pl.when(goes_down)
        def _():
            down_copy(t).wait_send()

        for d in range(1, ny):
            y_copy(t, d).wait_send()

    def multiply(t):
        _, half, _, kk, f = place(t)
        for d in range(1, ny):
            y_arrival(t, d).wait_recv()

        @pl.when(half == 0)
        def _():
            load(f).wait()

        def dot(a, b):
            return jnp.dot(a, b, preferred_element_type=jnp.float32)

        tile = min(256, width)

        @pl.loop(0, width // tile)
        def _(j):
            columns = pl.ds(pl.multiple_of(j * tile, tile), tile)
            real, imag = None, None
            for b in range(ny):
                depth = slice(b * width, (b + 1) * width)
                ur, ui = upper[b, t, 0], upper[b, t, 1]
                dr, di = data[f, 0, depth, columns], data[f, 1, depth, columns]
                re = dot(ur, dr) - dot(ui, di)
                im = dot(ur, di) + dot(ui, dr)
                real = re if real is None else real + re
                imag = im if imag is None else imag + im
            part[t, 0, :, columns] = real
            part[t, 1, :, columns] = imag

        @pl.when(kk != k)
        def _():
            pair_copy(t).start()

    def join(t):
        group, _, hh, kk, _ = place(t)

        @pl.when(kk == k)
        def _():
            pair_arrival(t).wait_recv()
            part[t] = part[t] + pair[group * nh + hh]

            @pl.when(hh != h)
            def _():
                far_copy(t).start()

    def finish(t):
        group, half, hh, kk, _ = place(t)

        @pl.when(kk != k)
        def _():
            pair_copy(t).wait_send()

        @pl.when((kk == k) & (hh != h))
        def _():
            far_copy(t).wait_send()

        @pl.when((kk == k) & (hh == h))
        def _():
            for d in range(nh - 1):
                far_arrival(t, d).wait_recv()
            real, imag = part[t, 0], part[t, 1]
            for d in range(nh - 1):
                real = real + far[d, group, 0]
                imag = imag + far[d, group, 1]
            j = lax.div(group, HALVES)
            wr, wi = wave[0, j], wave[1, j]
            where = pl.ds(pl.multiple_of(half * rows, rows), rows)
            out[0, j, where, :] = (-(wr * real - wi * imag)).astype(out.dtype)
            out[1, j, where, :] = (-(wr * imag + wi * real)).astype(out.dtype)

    def within(t, fn):
        @pl.when((t >= 0) & (t < chunks))
        def _():
            fn(t)

    late = chunks - 4

    @pl.loop(0, chunks + max(LAG, AHEAD))
    def _(t):
        within(t - AHEAD, sent)

        @pl.when((t >= 1) & (t + AHEAD - 1 < chunks))
        def _():
            start_source(t + AHEAD - 1)

        within(t, arrive)
        within(t - 1, multiply)

        @pl.when(t < late)
        def _():
            within(t - 5, join)

        @pl.when((t >= late) & (t < late + 3))
        def _():
            for i in range(2):
                join(2 * (t - late) + late - 5 + i)

        @pl.when(t >= late + 3)
        def _():
            within(t - 2, join)

        within(t - LAG, finish)


def local(nf, ncol, spectra, wavelet):
    _, freqs, shots, width = spectra.shape
    own = wavelet.shape[1]
    rows, chunks = NOUT // HALVES, freqs * HALVES
    ny, nh = ncol // nf, nf // 2
    block = (2, rows, width)
    dma = pltpu.SemaphoreType.DMA
    return pl.pallas_call(
        functools.partial(kernel, nf, ncol),
        out_shape=jax.ShapeDtypeStruct((2, own, NOUT, width), jnp.bfloat16),
        in_specs=[pl.BlockSpec(memory_space=pl.ANY), pl.BlockSpec(memory_space=pltpu.SMEM)],
        out_specs=pl.BlockSpec(memory_space=pltpu.VMEM),
        scratch_shapes=[
            pltpu.VMEM((ny, chunks) + block, jnp.bfloat16),
            pltpu.VMEM((freqs, 2, shots, width), jnp.bfloat16),
            pltpu.VMEM((chunks,) + block, jnp.float32),
            pltpu.VMEM((chunks // 2,) + block, jnp.float32),
            pltpu.VMEM((nh - 1, chunks // nf) + block, jnp.float32),
            dma((freqs,)),
            dma((chunks,)),
            dma((chunks,)),
            dma((chunks,)),
            dma((chunks,)),
            dma((ny - 1, chunks)),
            dma((ny - 1, chunks)),
            dma((chunks,)),
            dma((chunks // 2,)),
            dma((chunks,)),
            dma((nh - 1, chunks // nf)),
        ],
        compiler_params=pltpu.CompilerParams(
            collective_id=0, has_side_effects=True, vmem_limit_bytes=58 * 2**20
        ),
        cost_estimate=pl.CostEstimate(
            flops=16 * freqs * NOUT * shots * width // 2, bytes_accessed=4 * freqs * shots * width, transcendentals=0
        ),
    )(spectra, wavelet)


def solution(mesh):
    return jax.shard_map(
        functools.partial(local, mesh.shape["freq"], mesh.shape["col"]),
        mesh=mesh,
        in_specs=(P(None, None, "freq", "col"), P(None, "freq")),
        out_specs=P(None, "freq", None, "col"),
        check_vma=False,
    )
```

```python
import functools

import jax
import jax.numpy as jnp
from jax import lax
from jax.experimental import pallas as pl
from jax.experimental.pallas import tpu as pltpu
from jax.sharding import PartitionSpec as P

NOUT = 384
HALVES = 3
AHEAD = 12
LAG = 12
MESH = pl.DeviceIdType.MESH


def kernel(nf, ncol, spec, wave, out, upper, data, part, pair, far, data_sem, src_send, col_recv,
           up_send, down_send, y_send, y_recv, pair_send, pair_recv, far_send, far_recv):
    own = wave.shape[1]
    freqs, shots, width = spec.shape[1], spec.shape[2], spec.shape[3]
    ny = ncol // nf
    nz, nh = nf, nf // 2
    rows = NOUT // HALVES
    chunks = freqs * HALVES
    r, c = lax.axis_index("freq"), lax.axis_index("col")
    z, y = lax.div(c, ny), lax.rem(c, ny)
    h, k = lax.div(r, 2), lax.rem(r, 2)

    def at(freq, col):
        return {"freq": freq, "col": col}

    barrier = pltpu.get_barrier_semaphore()
    for d in range(1, nf):
        pl.semaphore_signal(barrier, inc=1, device_id=at(lax.rem(r + d, nf), c), device_id_type=MESH)
    for d in range(1, ny):
        pl.semaphore_signal(
            barrier, inc=1, device_id=at(r, z * ny + lax.rem(y + d, ny)), device_id_type=MESH
        )

    @pl.when(z > 0)
    def _():
        pl.semaphore_signal(barrier, inc=1, device_id=at(r, c - ny), device_id_type=MESH)

    @pl.when(z < nz - 1)
    def _():
        pl.semaphore_signal(barrier, inc=1, device_id=at(r, c + ny), device_id_type=MESH)

    def place(t):
        group, spot = lax.div(t, nf), lax.rem(t, nf)
        hh, kk = lax.rem(spot, nh), lax.div(spot, nh)
        f = (hh * 2 + kk) * own + lax.div(group, HALVES)
        return group, lax.rem(group, HALVES), hh, kk, f

    def source(t):
        _, half, _, _, f = place(t)
        return spec.at[:, f, pl.ds(pl.multiple_of(half * rows, rows), rows), :]

    def remote(src, dst, send, recv, device):
        return pltpu.make_async_remote_copy(
            src_ref=src, dst_ref=dst, send_sem=send, recv_sem=recv, device_id=device, device_id_type=MESH
        )

    def local_copy(t):
        return pltpu.make_async_copy(source(t), upper.at[y, t], col_recv.at[t])

    def source_copy(t):
        return remote(source(t), upper.at[y, t], src_send.at[t], col_recv.at[t], at(z, c))

    def up_copy(t):
        return remote(upper.at[y, t], upper.at[y, t], up_send.at[t], col_recv.at[t], at(r, c + ny))

    def down_copy(t):
        return remote(upper.at[y, t], upper.at[y, t], down_send.at[t], col_recv.at[t], at(r, c - ny))

    def y_copy(t, d):
        to = at(r, z * ny + lax.rem(y + d, ny))
        return remote(upper.at[y, t], upper.at[y, t], y_send.at[d - 1, t], y_recv.at[d - 1, t], to)

    def y_arrival(t, d):
        origin = lax.rem(y - d + ny, ny)
        block = upper.at[origin, t]
        return remote(block, block, y_send.at[d - 1, t], y_recv.at[d - 1, t], at(r, z * ny + origin))

    def pair_copy(t):
        group, _, hh, kk, _ = place(t)
        slot = group * nh + hh
        return remote(part.at[t], pair.at[slot], pair_send.at[t], pair_recv.at[slot], at(h * 2 + kk, c))

    def pair_arrival(t):
        group, _, hh, _, _ = place(t)
        slot = group * nh + hh
        return remote(part.at[t], pair.at[slot], pair_send.at[t], pair_recv.at[slot], at(h * 2 + 1 - k, c))

    def far_copy(t):
        group, _, hh, kk, _ = place(t)
        d = lax.rem(h - hh + nh, nh) - 1
        return remote(part.at[t], far.at[d, group], far_send.at[t], far_recv.at[d, group], at(hh * 2 + kk, c))

    def far_arrival(t, d):
        group, _, hh, kk, _ = place(t)
        origin = lax.rem(h + d + 1, nh) * 2 + k
        return remote(part.at[t], far.at[d, group], far_send.at[t], far_recv.at[d, group], at(origin, c))

    local_root = (r == 0) & (z == 0)
    sends_source = (r == 0) & (z > 0)
    goes_up = (z >= r) & (z < nz - 1)
    goes_down = (z <= r) & (z > 0)

    def start_source(t):
        @pl.when(local_root)
        def _():
            local_copy(t).start()

        @pl.when(sends_source)
        def _():
            source_copy(t).start()

    count = (nf - 1) + (ny - 1) + (z > 0).astype(jnp.int32) + (z < nz - 1).astype(jnp.int32)
    pl.semaphore_wait(barrier, count)

    for t in range(AHEAD):
        start_source(t)

    def load(f):
        return pltpu.make_async_copy(spec.at[:, f], data.at[f], data_sem.at[f])

    @pl.loop(0, freqs)
    def _(i):
        load(place(lax.rem(i, nf) + lax.div(i, nf) * nf * HALVES)[4]).start()

    def arrive(t):
        @pl.when(local_root)
        def _():
            local_copy(t).wait()

        @pl.when(jnp.logical_not(local_root))
        def _():
            down_copy(t).wait_recv()

        @pl.when(goes_up)
        def _():
            up_copy(t).start()

        @pl.when(goes_down)
        def _():
            down_copy(t).start()

        for d in range(1, ny):
            y_copy(t, d).start()

    def sent(t):
        @pl.when(sends_source)
        def _():
            source_copy(t).wait_send()

        @pl.when(goes_up)
        def _():
            up_copy(t).wait_send()

        @pl.when(goes_down)
        def _():
            down_copy(t).wait_send()

        for d in range(1, ny):
            y_copy(t, d).wait_send()

    def multiply(t):
        _, half, _, kk, f = place(t)
        for d in range(1, ny):
            y_arrival(t, d).wait_recv()

        @pl.when(half == 0)
        def _():
            load(f).wait()

        def dot(a, b):
            return jnp.dot(a, b, preferred_element_type=jnp.float32)

        tile = min(256, width)

        @pl.loop(0, width // tile)
        def _(j):
            columns = pl.ds(pl.multiple_of(j * tile, tile), tile)
            real, imag = None, None
            for b in range(ny):
                depth = slice(b * width, (b + 1) * width)
                ur, ui = upper[b, t, 0], upper[b, t, 1]
                dr, di = data[f, 0, depth, columns], data[f, 1, depth, columns]
                re = dot(ur, dr) - dot(ui, di)
                im = dot(ur, di) + dot(ui, dr)
                real = re if real is None else real + re
                imag = im if imag is None else imag + im
            part[t, 0, :, columns] = real
            part[t, 1, :, columns] = imag

        @pl.when(kk != k)
        def _():
            pair_copy(t).start()

    def join(t):
        group, _, hh, kk, _ = place(t)

        @pl.when(kk == k)
        def _():
            pair_arrival(t).wait_recv()
            part[t] = part[t] + pair[group * nh + hh]

            @pl.when(hh != h)
            def _():
                far_copy(t).start()

    def finish(t):
        group, half, hh, kk, _ = place(t)

        @pl.when(kk != k)
        def _():
            pair_copy(t).wait_send()

        @pl.when((kk == k) & (hh != h))
        def _():
            far_copy(t).wait_send()

        @pl.when((kk == k) & (hh == h))
        def _():
            for d in range(nh - 1):
                far_arrival(t, d).wait_recv()
            real, imag = part[t, 0], part[t, 1]
            for d in range(nh - 1):
                real = real + far[d, group, 0]
                imag = imag + far[d, group, 1]
            j = lax.div(group, HALVES)
            wr, wi = wave[0, j], wave[1, j]
            where = pl.ds(pl.multiple_of(half * rows, rows), rows)
            out[0, j, where, :] = (-(wr * real - wi * imag)).astype(out.dtype)
            out[1, j, where, :] = (-(wr * imag + wi * real)).astype(out.dtype)

    def within(t, fn):
        @pl.when((t >= 0) & (t < chunks))
        def _():
            fn(t)

    late = chunks - 4

    @pl.loop(0, chunks + max(LAG, AHEAD))
    def _(t):
        within(t - AHEAD, sent)

        @pl.when((t >= 1) & (t + AHEAD - 1 < chunks))
        def _():
            start_source(t + AHEAD - 1)

        within(t, arrive)
        within(t - 1, multiply)

        @pl.when(t < late)
        def _():
            within(t - 5, join)

        @pl.when((t >= late) & (t < late + 3))
        def _():
            for i in range(2):
                join(2 * (t - late) + late - 5 + i)

        @pl.when(t >= late + 3)
        def _():
            within(t - 2, join)

        within(t - LAG, finish)


def local(nf, ncol, spectra, wavelet):
    _, freqs, shots, width = spectra.shape
    own = wavelet.shape[1]
    rows, chunks = NOUT // HALVES, freqs * HALVES
    ny, nh = ncol // nf, nf // 2
    block = (2, rows, width)
    dma = pltpu.SemaphoreType.DMA
    return pl.pallas_call(
        functools.partial(kernel, nf, ncol),
        out_shape=jax.ShapeDtypeStruct((2, own, NOUT, width), jnp.bfloat16),
        in_specs=[pl.BlockSpec(memory_space=pl.ANY), pl.BlockSpec(memory_space=pltpu.SMEM)],
        out_specs=pl.BlockSpec(memory_space=pltpu.VMEM),
        scratch_shapes=[
            pltpu.VMEM((ny, chunks) + block, jnp.bfloat16),
            pltpu.VMEM((freqs, 2, shots, width), jnp.bfloat16),
            pltpu.VMEM((chunks,) + block, jnp.float32),
            pltpu.VMEM((chunks // 2,) + block, jnp.float32),
            pltpu.VMEM((nh - 1, chunks // nf) + block, jnp.float32),
            dma((freqs,)),
            dma((chunks,)),
            dma((chunks,)),
            dma((chunks,)),
            dma((chunks,)),
            dma((ny - 1, chunks)),
            dma((ny - 1, chunks)),
            dma((chunks,)),
            dma((chunks // 2,)),
            dma((chunks,)),
            dma((nh - 1, chunks // nf)),
        ],
        compiler_params=pltpu.CompilerParams(
            collective_id=0, has_side_effects=True, vmem_limit_bytes=58 * 2**20
        ),
        cost_estimate=pl.CostEstimate(
            flops=16 * freqs * NOUT * shots * width // 2, bytes_accessed=4 * freqs * shots * width, transcendentals=0
        ),
    )(spectra, wavelet)


def solution(mesh):
    return jax.shard_map(
        functools.partial(local, mesh.shape["freq"], mesh.shape["col"]),
        mesh=mesh,
        in_specs=(P(None, None, "freq", "col"), P(None, "freq")),
        out_specs=P(None, "freq", None, "col"),
        check_vma=False,
    )
```
